256 devices in a mesh: fsdp: 32 (over x, z), rep: 8 (over y, core).
Axes of the slice: x: 4, y: 4, z: 8, core: 2. Of those that a mesh axis runs over, the one named last changes fastest.
Arguments:
- hidden: bfloat16 [4096, 16384], P('fsdp', 'rep'), may hold values from -6 to 6
- weight: bfloat16 [16384, 4096], P('fsdp', 'rep'), may hold values from -0.046875 to 0.046875
- gradient: bfloat16 [16384, 4096], P('fsdp', 'rep')
- stats_left: float32 [16384, 4096], P('fsdp', 'rep'), as said below
- stats_right: float32 [16384, 4096], P('fsdp', 'rep'), as said below
- root_left: float32 [16384, 4096], P('fsdp', 'rep'), as said below
- root_right: float32 [16384, 4096], P('fsdp', 'rep'), as said below
- due_rows: int32 [16, 8], replicated, may hold values from 0 to 31, as said below
Outputs:
- left_stats: float32 [16384, 4096], P('fsdp', 'rep')
- right_stats: float32 [16384, 4096], P('fsdp', 'rep')
- update: bfloat16 [16384, 4096], P('fsdp', 'rep')
- projected: bfloat16 [4096, 4096], P('fsdp', 'rep')
The draws below stay inside these ranges and needn't reach their ends.
Inputs may be any that keep to these rules, and one draw needn't show every extreme that they name: `due_rows`: entry [i, j] is i or i + 16: of the blocks in rows i and i + 16 of block column j exactly that one is due. `stats_left`: each block is symmetric with a positive diagonal that exceeds the sum of magnitudes of its row's other entries. `stats_right`: each block is symmetric with a positive diagonal that exceeds the sum of magnitudes of its row's other entries. `root_left`: each block is symmetric with a positive diagonal that exceeds the sum of magnitudes of its row's other entries. `root_right`: each block is symmetric with a positive diagonal that exceeds the sum of magnitudes of its row's other entries.
All inputs are finite; a program needn't handle non-finite values.
Results may differ from the reference program's by a relative error of at most 0.0053.
Values may be sent and summed in bfloat16 or wider, within the bound.
No kernel may reach another device: no remote copies, remote signals or barrier semaphores. Data moves between devices by JAX's collectives and lax.ppermute only.
A program may use at most 128 MiB of HBM per device.

```python
import jax
import jax.numpy as jnp
from jax import lax

B = 512
ITERS = 2
FF_W = 16384
D_W = 4096
TOKENS = 4096
N_FSDP = 32
N_REP = 8


def dominant_blocks(key, lowest, highest, spread_ratio):
    key_diag, key_off = jax.random.split(key)
    diagonal = jnp.exp(jax.random.uniform(key_diag, (N_FSDP, N_REP, B), jnp.float32, jnp.log(lowest), jnp.log(highest)))
    uniform_draw = jax.random.uniform(key_off, (N_FSDP, N_REP, B, B), jnp.float32, -1.0, 1.0)
    symmetric = 0.5 * (uniform_draw + jnp.swapaxes(uniform_draw, 2, 3))
    limit_mag = jnp.minimum(diagonal[:, :, :, None], diagonal[:, :, None, :]) * (spread_ratio / (B - 1))
    on_diagonal = lax.broadcasted_iota(jnp.int32, (B, B), 0) == lax.broadcasted_iota(jnp.int32, (B, B), 1)
    blocks = jnp.where(on_diagonal, diagonal[:, :, :, None], symmetric * limit_mag)
    return blocks.transpose(0, 2, 1, 3).reshape(N_FSDP * B, N_REP * B)


def draw_stats_left(key, part):
    key = jax.random.fold_in(key, 11)
    return dominant_blocks(key, 0.3, 3.0, 0.9)


def draw_stats_right(key, part):
    key = jax.random.fold_in(key, 13)
    return dominant_blocks(key, 0.3, 3.0, 0.9)


def draw_root_left(key, part):
    key = jax.random.fold_in(key, 17)
    return dominant_blocks(key, 0.5, 2.0, 0.9)


def draw_root_right(key, part):
    key = jax.random.fold_in(key, 19)
    return dominant_blocks(key, 0.5, 2.0, 0.9)


def draw_gradient(key, part):
    key = jax.random.fold_in(key, 23)
    key_rows, key_cols, key_vals = jax.random.split(key, 3)
    row_scale = jnp.exp(jax.random.uniform(key_rows, (FF_W, 1), jnp.float32, jnp.log(0.3), jnp.log(3.0)))
    col_scale = jnp.exp(jax.random.uniform(key_cols, (1, D_W), jnp.float32, jnp.log(0.3), jnp.log(3.0)))
    entries = jax.random.uniform(key_vals, (FF_W, D_W), jnp.float32, -1.7, 1.7)
    return (entries * row_scale * col_scale).astype(jnp.bfloat16)


def draw_due_rows(key, part):
    key = jax.random.fold_in(key, 29)
    half_rows = N_FSDP // 2
    upper_pick = jax.random.randint(key, (half_rows, N_REP), 0, 2)
    row_ids = lax.broadcasted_iota(jnp.int32, (half_rows, N_REP), 0)
    col_ids = lax.broadcasted_iota(jnp.int32, (half_rows, N_REP), 1)
    upper_pick = jnp.where((row_ids == 0) & (col_ids == 0), 0, upper_pick)
    upper_pick = jnp.where((row_ids == half_rows - 1) & (col_ids == 0), 1, upper_pick)
    return (row_ids + upper_pick * half_rows).astype(jnp.int32)


def block_scale(key, dims, pieces, low, high):
    def one(position, parts):
        draws = jax.random.uniform(jax.random.fold_in(jax.random.fold_in(key, 6), position), (parts,), jnp.float32, low / len(pieces), high / len(pieces))
        return jnp.repeat(jnp.exp(draws), dims[position] // parts).reshape((-1,) + (1,) * (len(dims) - position - 1))

    loudness = one(*pieces[0])
    for cut in pieces[1:]:
        loudness = loudness * one(*cut)
    return loudness


def bell_draw(rng, shape, spread, bound, cuts=(), kind=jnp.bfloat16):
    values = spread * jax.random.normal(rng, shape, jnp.float32)
    if cuts:
        values = values * block_scale(rng, shape, cuts, -0.22, 0.18)
    return jnp.clip(values, -bound, bound).astype(kind)


def setup_inputs(seed: int = 0) -> dict:
    key_list = jax.random.split(jax.random.key(seed), 9)
    return {
        "hidden": bell_draw(key_list[0], (TOKENS, FF_W), 1.0, 6.0, ((0, 32), (1, 8))),
        "weight": bell_draw(key_list[1], (FF_W, D_W), FF_W ** -0.5, 0.046875, ((0, 32), (1, 8))),
        "gradient": draw_gradient(jax.random.fold_in(key_list[8], 71), 0),
        "stats_left": draw_stats_left(jax.random.fold_in(key_list[8], 71), 0),
        "stats_right": draw_stats_right(jax.random.fold_in(key_list[8], 71), 0),
        "root_left": draw_root_left(jax.random.fold_in(key_list[8], 71), 0),
        "root_right": draw_root_right(jax.random.fold_in(key_list[8], 71), 0),
        "due_rows": draw_due_rows(jax.random.fold_in(key_list[8], 71), 0),
    }


ridge_value = 0.001
keep_share = 0.75
step_size = 0.003
graft_floor = 1e-06

def matmul(first, second):
    return jnp.dot(first, second, precision=lax.Precision.HIGHEST, preferred_element_type=jnp.float32)

def inverse_root(statistic, turns):
    block_size = statistic.shape[-1]
    identity_matrix = jnp.eye(block_size, dtype=jnp.float32)
    shifted = statistic + ridge_value * identity_matrix
    norm_scale = jnp.sqrt(jnp.sum(shifted * shifted))
    current = shifted / norm_scale
    result = identity_matrix * norm_scale ** (-0.25)
    for iteration in range(turns):
        factor = (5.0 * identity_matrix - current) / 4.0
        result = matmul(result, factor)
        square = matmul(factor, factor)
        fourth = matmul(square, square)
        current = matmul(fourth, current)
    return result

def to_blocks(whole_matrix):
    return whole_matrix.reshape(N_FSDP, B, N_REP, B).transpose(0, 2, 1, 3).reshape(N_FSDP * N_REP, B, B)

def from_blocks(blocks):
    return blocks.reshape(N_FSDP, N_REP, B, B).transpose(0, 2, 1, 3).reshape(N_FSDP * B, N_REP * B)

def block_step(items):
    gradient_block, left_stats, right_stats, left_root, right_root, is_due = items
    block_size = gradient_block.shape[0]
    gram_left = jnp.dot(gradient_block, gradient_block.T, preferred_element_type=jnp.float32) / block_size
    gram_right = jnp.dot(gradient_block.T, gradient_block, preferred_element_type=jnp.float32) / block_size
    new_left = keep_share * left_stats + (1.0 - keep_share) * gram_left
    new_right = keep_share * right_stats + (1.0 - keep_share) * gram_right
    left_used = jnp.where(is_due, inverse_root(new_left, ITERS), left_root)
    right_used = jnp.where(is_due, inverse_root(new_right, ITERS), right_root)
    gradient_wide = gradient_block.astype(jnp.float32)
    conditioned = matmul(matmul(left_used, gradient_wide), right_used)
    graft = jnp.sqrt(jnp.mean(gradient_wide * gradient_wide)) / jnp.sqrt(jnp.mean(conditioned * conditioned) + graft_floor)
    update = (conditioned * graft).astype(jnp.bfloat16)
    return (new_left, new_right, update)

def reference(hidden, weight, gradient, stats_left, stats_right, root_left, root_right, due_rows):
    half_rows = N_FSDP // 2
    row_ids = jnp.arange(N_FSDP, dtype=jnp.int32)
    picked = due_rows[row_ids % half_rows, :]
    due_flags = (picked == row_ids[:, None]).reshape(N_FSDP * N_REP)
    left_new, right_new, updates = lax.map(block_step, (to_blocks(gradient), to_blocks(stats_left), to_blocks(stats_right), to_blocks(root_left), to_blocks(root_right), due_flags))
    update = from_blocks(updates)
    stored = lax.optimization_barrier(update)
    new_weight = (weight.astype(jnp.float32) - step_size * stored.astype(jnp.float32)).astype(jnp.bfloat16)
    projected = jnp.dot(hidden, new_weight, preferred_element_type=jnp.float32).astype(jnp.bfloat16)
    return (from_blocks(left_new), from_blocks(right_new), update, projected)
```

```python
import jax
import jax.numpy as jnp
from jax import lax
from jax.experimental import pallas as pl
from jax.experimental.pallas import tpu as pltpu
from jax.sharding import Mesh, PartitionSpec as P

BLOCK = 512
ROWS = 128
RIDGE = 0.001
KEEP = 0.75
STEP = 0.003
FLOOR = 1e-06
F32 = jnp.float32
BF16 = jnp.bfloat16
HBM = pl.BlockSpec(memory_space=pltpu.HBM)
VMEM = pl.BlockSpec(memory_space=pltpu.VMEM)


def vmem(one):
    return pltpu.with_memory_space_constraint(one, pltpu.VMEM)


def hbm(one):
    return pltpu.with_memory_space_constraint(one, pltpu.HBM)


def mm(first, second):
    return jnp.dot(first, second, preferred_element_type=F32)


def diagonal_mask():
    rows = lax.broadcasted_iota(jnp.int32, (BLOCK, BLOCK), 0)
    cols = lax.broadcasted_iota(jnp.int32, (BLOCK, BLOCK), 1)
    return rows == cols


def total(values):
    return jnp.sum(jnp.sum(values, axis=0, keepdims=True), axis=1, keepdims=True)


def fresh_root(statistic):
    on_diagonal = diagonal_mask()
    shifted = statistic + jnp.where(on_diagonal, RIDGE, 0.0)
    norm = jnp.sqrt(total(shifted * shifted))
    e1 = shifted * (0.2 / norm)
    e1_low = e1.astype(BF16)
    e2 = mm(e1_low, e1_low)
    e3 = mm(e2.astype(BF16), e1_low)
    e3_low = e3.astype(BF16)
    tail = mm(e3_low, (5.0 * e2 - 10.0 * e1 - e3).astype(BF16))
    a, b = 1.25**2, 1.25**6
    series = -(a + b) * e1 + (5.0 * b) * e2 - (10.0 * b) * e3 - b * tail
    return (series + jnp.where(on_diagonal, a, 0.0)) * lax.rsqrt(jnp.sqrt(norm))


def step_kernel(
    due_hbm, grad_hbm, weight_hbm, sl_hbm, sr_hbm, rl_hbm, rr_hbm,
    nl_hbm, nr_hbm, update_ref, new_ref,
    due_ref, grad_ref, weight_ref, sl, sr, left, right, sems,
):
    copy = pltpu.make_async_copy
    get_due = copy(due_hbm, due_ref, sems.at[0])
    get_grad = copy(grad_hbm, grad_ref, sems.at[1])
    get_weight = copy(weight_hbm, weight_ref, sems.at[2])
    get_sl = copy(sl_hbm, sl, sems.at[3])
    get_sr = copy(sr_hbm, sr, sems.at[4])
    get_rl = copy(rl_hbm, left, sems.at[5])
    get_rr = copy(rr_hbm, right, sems.at[6])
    put_sl = copy(sl, nl_hbm, sems.at[7])
    put_sr = copy(sr, nr_hbm, sems.at[8])
    get_due.start()
    get_grad.start()
    get_sl.start()
    get_sr.start()
    get_weight.start()
    row = lax.axis_index("x") * 8 + lax.axis_index("z")
    col = lax.axis_index("y") * 2 + lax.axis_index("core")
    get_due.wait()
    due = due_ref[col, row % 16] == row

    @pl.when(jnp.logical_not(due))
    def _():
        get_rl.start()
        get_rr.start()

    get_grad.wait()
    grad = grad_ref[...]
    scale = (1.0 - KEEP) / BLOCK
    gram = lax.dot_general(grad, grad, (((1,), (1,)), ((), ())), preferred_element_type=F32)
    get_sl.wait()
    sl[...] = KEEP * sl[...] + scale * gram
    put_sl.start()
    gram = lax.dot_general(grad, grad, (((0,), (0,)), ((), ())), preferred_element_type=F32)
    get_sr.wait()
    sr[...] = KEEP * sr[...] + scale * gram
    put_sr.start()

    @pl.when(due)
    def _():
        left[...] = fresh_root(sl[...])
        right[...] = fresh_root(sr[...])

    @pl.when(jnp.logical_not(due))
    def _():
        get_rl.wait()
        get_rr.wait()

    on_diagonal = diagonal_mask()
    wide = grad.astype(F32)
    used = left[...]
    diag = jnp.sum(jnp.where(on_diagonal, used, 0.0), axis=1, keepdims=True)
    half = diag * wide + mm(jnp.where(on_diagonal, 0.0, used).astype(BF16), grad)
    used = right[...]
    diag = jnp.sum(jnp.where(on_diagonal, used, 0.0), axis=0, keepdims=True)
    cond = half * diag + mm(half.astype(BF16), jnp.where(on_diagonal, 0.0, used).astype(BF16))
    count = 1.0 / (BLOCK * BLOCK)
    graft = jnp.sqrt(total(wide * wide) * count) / jnp.sqrt(total(cond * cond) * count + FLOOR)
    update = (cond * graft).astype(BF16)
    update_ref[...] = update
    get_weight.wait()
    new_ref[...] = (weight_ref[...].astype(F32) - STEP * update.astype(F32)).astype(BF16)
    put_sl.wait()
    put_sr.wait()


def block_step(*operands):
    wide = jax.ShapeDtypeStruct((BLOCK, BLOCK), F32)
    low = jax.ShapeDtypeStruct((BLOCK, BLOCK), BF16)
    return pl.pallas_call(
        step_kernel,
        out_shape=(wide, wide, low, pltpu.VMEM((BLOCK, BLOCK), BF16)),
        in_specs=[HBM] * 7,
        out_specs=(HBM, HBM, VMEM, VMEM),
        scratch_shapes=[pltpu.SMEM((8, 16), jnp.int32)]
        + [pltpu.VMEM((BLOCK, BLOCK), BF16) for _ in range(2)]
        + [pltpu.VMEM((BLOCK, BLOCK), F32) for _ in range(4)]
        + [pltpu.SemaphoreType.DMA((9,))],
        compiler_params=pltpu.CompilerParams(vmem_limit_bytes=24 * 1024 * 1024),
        cost_estimate=pl.CostEstimate(
            flops=2 * 30 * BLOCK**3, bytes_accessed=9 * 1024 * 1024, transcendentals=0
        ),
        name="block_step",
    )(*[hbm(one) for one in operands])


def split_kernel(hidden, *outs):
    place = lax.axis_index("z") % 4
    for shift in range(4):
        start = pl.multiple_of(((place + shift) % 4) * BLOCK, BLOCK)
        outs[shift][...] = hidden[:, pl.ds(start, BLOCK)]


def split_hidden(hidden):
    part = pltpu.VMEM((ROWS, BLOCK), BF16)
    return pl.pallas_call(
        split_kernel,
        out_shape=(part,) * 4,
        in_specs=[VMEM],
        out_specs=(VMEM,) * 4,
        compiler_params=pltpu.CompilerParams(vmem_limit_bytes=4 * 1024 * 1024),
        cost_estimate=pl.CostEstimate(flops=0, bytes_accessed=1024 * 1024, transcendentals=0),
        name="split_hidden",
    )(hidden)


def project_kernel(*refs):
    near, far, weights, outs = refs[0:4], refs[4:8], refs[8:12], refs[12:20]
    placed, sems = refs[20:22]
    x, z = lax.axis_index("x"), lax.axis_index("z")
    y, core = lax.axis_index("y"), lax.axis_index("core")
    copies = [
        pltpu.make_async_copy(weights[i], placed.at[(x + i) % 4], sems.at[i]) for i in range(4)
    ]
    for one in copies:
        one.start()
    for one in copies:
        one.wait()
    sides = []
    for blocks in (near, far):
        acc = mm(blocks[0][...], placed[y])
        for j in range(1, 4):
            acc += mm(blocks[j][...], placed[(y + j) % 4])
        sides.append(acc)
    for s in range(8):
        piece = -s % 4
        rows = slice(piece * ROWS, (piece + 1) * ROWS)
        is_near = ((z + s) % 8) // 4 == core
        outs[s][...] = jnp.where(is_near, sides[0][rows], sides[1][rows]).astype(outs[s].dtype)


def project(near, far, weights):
    part = pltpu.VMEM((ROWS, BLOCK), BF16)
    return pl.pallas_call(
        project_kernel,
        out_shape=(pltpu.VMEM((ROWS, BLOCK), F32),) + (part,) * 7,
        in_specs=[VMEM] * 12,
        out_specs=(VMEM,) * 8,
        scratch_shapes=[pltpu.VMEM((4, BLOCK, BLOCK), BF16), pltpu.SemaphoreType.DMA((4,))],
        compiler_params=pltpu.CompilerParams(vmem_limit_bytes=20 * 1024 * 1024),
        cost_estimate=pl.CostEstimate(
            flops=2 * 1024 * 2048 * BLOCK, bytes_accessed=8 * 1024 * 1024, transcendentals=0
        ),
        name="project",
    )(*[vmem(one) for one in (*near, *far, *weights)])


def ring(size, shift):
    return [((i + shift) % size, i) for i in range(size)]


def body(hidden, weight, gradient, stats_left, stats_right, root_left, root_right, due_rows):
    pieces = split_hidden(hidden)
    tokens = []
    for shift in range(4):
        perm = []
        for z in range(8):
            for core in range(2):
                perm.append((z * 2 + core, (core * 4 + (z % 4 + shift) % 4) * 2 + z // 4))
        tokens.append(lax.ppermute(pieces[shift], ("z", "core"), perm))
    new_left, new_right, update, new_weight = block_step(
        due_rows.T, gradient, weight, stats_left, stats_right, root_left, root_right
    )
    *tokens, new_weight = lax.optimization_barrier((*tokens, new_weight))
    own = jnp.concatenate(tokens, axis=0)
    near = [own] + [lax.ppermute(own, "y", ring(4, j)) for j in (1, 2, 3)]
    weights = [new_weight] + [lax.ppermute(new_weight, "x", ring(4, i)) for i in (1, 2, 3)]
    far = [lax.ppermute(one, "core", ring(2, 1)) for one in near]
    parts = project(near, far, weights)
    projected = parts[0]
    for s in (4, 3, 5, 2, 6, 1, 7):
        projected += lax.ppermute(parts[s], "z", ring(8, 8 - s)).astype(F32)
    return (new_left, new_right, update, projected.astype(BF16))


def solution(mesh):
    grid = Mesh(mesh.devices.reshape(4, 8, 4, 2), ("x", "z", "y", "core"))
    spec = P(("x", "z"), ("y", "core"))
    return jax.shard_map(
        body,
        mesh=grid,
        in_specs=(spec,) * 7 + (P(),),
        out_specs=(spec,) * 4,
        check_vma=False,
    )
```

```python
import jax
import jax.numpy as jnp
from jax import lax
from jax.experimental import pallas as pl
from jax.experimental.pallas import tpu as pltpu
from jax.sharding import Mesh, PartitionSpec as P

BLOCK = 512
HALF = 256
ROWS = 128
RIDGE = 0.001
KEEP = 0.75
STEP = 0.003
FLOOR = 1e-06
F32 = jnp.float32
BF16 = jnp.bfloat16
HBM = pl.BlockSpec(memory_space=pltpu.HBM)
VMEM = pl.BlockSpec(memory_space=pltpu.VMEM)


def vmem(one):
    return pltpu.with_memory_space_constraint(one, pltpu.VMEM)


def hbm(one):
    return pltpu.with_memory_space_constraint(one, pltpu.HBM)


def mm(first, second):
    return jnp.dot(first, second, preferred_element_type=F32)


def diagonal_mask():
    rows = lax.broadcasted_iota(jnp.int32, (BLOCK, BLOCK), 0)
    cols = lax.broadcasted_iota(jnp.int32, (BLOCK, BLOCK), 1)
    return rows == cols


def total(values):
    return jnp.sum(jnp.sum(values, axis=0, keepdims=True), axis=1, keepdims=True)


def fresh_root(statistic):
    on_diagonal = diagonal_mask()
    shifted = statistic + jnp.where(on_diagonal, RIDGE, 0.0)
    norm = jnp.sqrt(total(shifted * shifted))
    e1 = shifted * (0.2 / norm)
    e1_low = e1.astype(BF16)
    e2 = mm(e1_low, e1_low)
    e3 = mm(e2.astype(BF16), e1_low)
    e3_low = e3.astype(BF16)
    tail = mm(e3_low, (5.0 * e2 - 10.0 * e1 - e3).astype(BF16))
    a, b = 1.25**2, 1.25**6
    series = -(a + b) * e1 + (5.0 * b) * e2 - (10.0 * b) * e3 - b * tail
    return (series + jnp.where(on_diagonal, a, 0.0)) * lax.rsqrt(jnp.sqrt(norm))


def step_kernel(
    due_hbm, grad_hbm, weight_hbm, sl_hbm, sr_hbm, rl_hbm, rr_hbm,
    nl_hbm, nr_hbm, update_ref, new_ref,
    due_ref, grad_ref, weight_ref, sl, sr, left, right, sems,
):
    copy = pltpu.make_async_copy
    get_due = copy(due_hbm, due_ref, sems.at[0])
    get_grad = copy(grad_hbm, grad_ref, sems.at[1])
    get_weight = copy(weight_hbm, weight_ref, sems.at[2])
    get_sl = copy(sl_hbm, sl, sems.at[3])
    get_sr = copy(sr_hbm, sr, sems.at[4])
    get_rl = copy(rl_hbm, left, sems.at[5])
    get_rr = copy(rr_hbm, right, sems.at[6])
    put_sl = copy(sl, nl_hbm, sems.at[7])
    put_sr = copy(sr, nr_hbm, sems.at[8])
    get_due.start()
    get_grad.start()
    get_sl.start()
    get_sr.start()
    get_weight.start()
    row = lax.axis_index("x") * 8 + lax.axis_index("z")
    col = lax.axis_index("y") * 2 + lax.axis_index("core")
    get_due.wait()
    due = due_ref[col, row % 16] == row

    @pl.when(jnp.logical_not(due))
    def _():
        get_rl.start()
        get_rr.start()

    get_grad.wait()
    grad = grad_ref[...]
    scale = (1.0 - KEEP) / BLOCK
    gram = lax.dot_general(grad, grad, (((1,), (1,)), ((), ())), preferred_element_type=F32)
    get_sl.wait()
    sl[...] = KEEP * sl[...] + scale * gram
    put_sl.start()
    gram = lax.dot_general(grad, grad, (((0,), (0,)), ((), ())), preferred_element_type=F32)
    get_sr.wait()
    sr[...] = KEEP * sr[...] + scale * gram
    put_sr.start()

    @pl.when(due)
    def _():
        left[...] = fresh_root(sl[...])
        right[...] = fresh_root(sr[...])

    @pl.when(jnp.logical_not(due))
    def _():
        get_rl.wait()
        get_rr.wait()

    on_diagonal = diagonal_mask()
    wide = grad.astype(F32)
    used = left[...]
    diag = jnp.sum(jnp.where(on_diagonal, used, 0.0), axis=1, keepdims=True)
    half = diag * wide + mm(jnp.where(on_diagonal, 0.0, used).astype(BF16), grad)
    used = right[...]
    diag = jnp.sum(jnp.where(on_diagonal, used, 0.0), axis=0, keepdims=True)
    cond = half * diag + mm(half.astype(BF16), jnp.where(on_diagonal, 0.0, used).astype(BF16))
    count = 1.0 / (BLOCK * BLOCK)
    graft = jnp.sqrt(total(wide * wide) * count) / jnp.sqrt(total(cond * cond) * count + FLOOR)
    update = (cond * graft).astype(BF16)
    update_ref[...] = update
    get_weight.wait()
    new_ref[...] = (weight_ref[...].astype(F32) - STEP * update.astype(F32)).astype(BF16)
    put_sl.wait()
    put_sr.wait()


def block_step(*operands):
    wide = jax.ShapeDtypeStruct((BLOCK, BLOCK), F32)
    low = jax.ShapeDtypeStruct((BLOCK, BLOCK), BF16)
    return pl.pallas_call(
        step_kernel,
        out_shape=(wide, wide, low, pltpu.VMEM((BLOCK, BLOCK), BF16)),
        in_specs=[HBM] * 7,
        out_specs=(HBM, HBM, VMEM, VMEM),
        scratch_shapes=[pltpu.SMEM((8, 16), jnp.int32)]
        + [pltpu.VMEM((BLOCK, BLOCK), BF16) for _ in range(2)]
        + [pltpu.VMEM((BLOCK, BLOCK), F32) for _ in range(4)]
        + [pltpu.SemaphoreType.DMA((9,))],
        compiler_params=pltpu.CompilerParams(vmem_limit_bytes=24 * 1024 * 1024),
        cost_estimate=pl.CostEstimate(
            flops=2 * 30 * BLOCK**3, bytes_accessed=9 * 1024 * 1024, transcendentals=0
        ),
        name="block_step",
    )(*[hbm(one) for one in operands])


def split_kernel(hidden, *outs):
    place = lax.axis_index("z") % 4
    for shift in range(4):
        start = pl.multiple_of(((place + shift) % 4) * BLOCK, BLOCK)
        outs[shift][...] = hidden[:, pl.ds(start, BLOCK)]


def split_hidden(hidden):
    part = pltpu.VMEM((ROWS, BLOCK), BF16)
    return pl.pallas_call(
        split_kernel,
        out_shape=(part,) * 4,
        in_specs=[VMEM],
        out_specs=(VMEM,) * 4,
        compiler_params=pltpu.CompilerParams(vmem_limit_bytes=4 * 1024 * 1024),
        cost_estimate=pl.CostEstimate(flops=0, bytes_accessed=1024 * 1024, transcendentals=0),
        name="split_hidden",
    )(hidden)


def project_kernel(*refs):
    near, far, weights, outs = refs[0:4], refs[4:8], refs[8:13], refs[13:21]
    placed, sems = refs[21:23]
    x, z = lax.axis_index("x"), lax.axis_index("z")
    y, core = lax.axis_index("y"), lax.axis_index("core")
    opposite = placed.at[(x + 2) % 4]
    homes = [
        placed.at[x],
        placed.at[(x + 1) % 4],
        opposite.at[pl.ds(0, HALF)],
        opposite.at[pl.ds(HALF, HALF)],
        placed.at[(x + 3) % 4],
    ]
    copies = [pltpu.make_async_copy(weights[i], homes[i], sems.at[i]) for i in range(5)]
    for one in copies:
        one.start()
    for one in copies:
        one.wait()
    sides = []
    for blocks in (near, far):
        acc = mm(blocks[0][...], placed[y])
        for j in range(1, 4):
            acc += mm(blocks[j][...], placed[(y + j) % 4])
        sides.append(acc)
    for s in range(8):
        piece = -s % 4
        rows = slice(piece * ROWS, (piece + 1) * ROWS)
        is_near = ((z + s) % 8) // 4 == core
        outs[s][...] = jnp.where(is_near, sides[0][rows], sides[1][rows]).astype(outs[s].dtype)


def project(near, far, weights):
    part = pltpu.VMEM((ROWS, BLOCK), BF16)
    return pl.pallas_call(
        project_kernel,
        out_shape=(pltpu.VMEM((ROWS, BLOCK), F32),) + (part,) * 7,
        in_specs=[VMEM] * 13,
        out_specs=(VMEM,) * 8,
        scratch_shapes=[pltpu.VMEM((4, BLOCK, BLOCK), BF16), pltpu.SemaphoreType.DMA((5,))],
        compiler_params=pltpu.CompilerParams(vmem_limit_bytes=20 * 1024 * 1024),
        cost_estimate=pl.CostEstimate(
            flops=2 * 1024 * 2048 * BLOCK, bytes_accessed=8 * 1024 * 1024, transcendentals=0
        ),
        name="project",
    )(*[vmem(one) for one in (*near, *far, *weights)])


def ring(size, shift):
    return [((i + shift) % size, i) for i in range(size)]


def add(first, second):
    return (first.astype(F32) + second.astype(F32)).astype(BF16)


def body(hidden, weight, gradient, stats_left, stats_right, root_left, root_right, due_rows):
    pieces = split_hidden(hidden)
    tokens = []
    for shift in range(4):
        perm = []
        for z in range(8):
            for core in range(2):
                perm.append((z * 2 + core, (core * 4 + (z % 4 + shift) % 4) * 2 + z // 4))
        tokens.append(lax.ppermute(pieces[shift], ("z", "core"), perm))
    new_left, new_right, update, new_weight = block_step(
        due_rows.T, gradient, weight, stats_left, stats_right, root_left, root_right
    )
    *tokens, new_weight = lax.optimization_barrier((*tokens, new_weight))
    own = jnp.concatenate(tokens, axis=0)
    near = [own] + [lax.ppermute(own, "y", ring(4, j)) for j in (1, 2, 3)]
    one, three = (lax.ppermute(new_weight, "x", ring(4, i)) for i in (1, 3))
    top = lax.ppermute(one[:HALF], "x", ring(4, 1))
    bottom = lax.ppermute(three[HALF:], "x", ring(4, 3))
    near[1], top, bottom = lax.optimization_barrier((near[1], top, bottom))
    weights = [new_weight, one, top, bottom, three]
    far = [lax.ppermute(piece, "core", ring(2, 1)) for piece in near]
    parts = project(near, far, weights)
    up, down = parts[3], parts[5]
    for near_up, near_down in ((parts[2], parts[6]), (parts[1], parts[7])):
        up = add(near_up, lax.ppermute(up, "z", ring(8, 7)))
        down = add(near_down, lax.ppermute(down, "z", ring(8, 1)))
    up, down = lax.ppermute(up, "z", ring(8, 7)), lax.ppermute(down, "z", ring(8, 1))
    far_sum = lax.ppermute(parts[4], "z", ring(8, 4))
    projected = parts[0] + up.astype(F32) + down.astype(F32) + far_sum.astype(F32)
    return (new_left, new_right, update, projected.astype(BF16))


def solution(mesh):
    grid = Mesh(mesh.devices.reshape(4, 8, 4, 2), ("x", "z", "y", "core"))
    spec = P(("x", "z"), ("y", "core"))
    return jax.shard_map(
        body,
        mesh=grid,
        in_specs=(spec,) * 7 + (P(),),
        out_specs=(spec,) * 4,
        check_vma=False,
    )
```

```python
import jax
import jax.numpy as jnp
from jax import lax
from jax.experimental import pallas as pl
from jax.experimental.pallas import tpu as pltpu
from jax.sharding import Mesh, PartitionSpec as P

BLOCK = 512
HALF = 256
ROWS = 128
RIDGE = 0.001
KEEP = 0.75
STEP = 0.003
FLOOR = 1e-06
F32 = jnp.float32
BF16 = jnp.bfloat16
HBM = pl.BlockSpec(memory_space=pltpu.HBM)
VMEM = pl.BlockSpec(memory_space=pltpu.VMEM)


def vmem(one):
    return pltpu.with_memory_space_constraint(one, pltpu.VMEM)


def hbm(one):
    return pltpu.with_memory_space_constraint(one, pltpu.HBM)


def mm(first, second):
    return jnp.dot(first, second, preferred_element_type=F32)


def total(values):
    return jnp.sum(jnp.sum(values, axis=0, keepdims=True), axis=1, keepdims=True)


def unit(size):
    rows = lax.broadcasted_iota(jnp.int32, (size, size), 0)
    cols = lax.broadcasted_iota(jnp.int32, (size, size), 1)
    return rows == cols


def tiles():
    return [(slice(i, i + ROWS), slice(i, i + ROWS)) for i in range(0, BLOCK, ROWS)]


def fresh_roots(statistics, scratch):
    diagonal = unit(ROWS)
    sides = range(len(statistics))
    norms = []
    for statistic in statistics:
        values = statistic[...]
        trace = sum(total(jnp.where(diagonal, statistic[tile], 0.0)) for tile in tiles())
        squares = total(values * values)
        norms.append(jnp.sqrt(squares + 2.0 * RIDGE * trace + BLOCK * RIDGE * RIDGE))
    for i in sides:
        shrink = 0.2 / norms[i]
        scratch[i][...] = statistics[i][...] * shrink
        for tile in tiles():
            scratch[i][tile] += jnp.where(diagonal, RIDGE * shrink, 0.0)
    low = [scratch[i][...].astype(BF16) for i in sides]
    e2 = [mm(low[i], low[i]) for i in sides]
    e3 = [mm(e2[i].astype(BF16), low[i]) for i in sides]
    inner = [(5.0 * e2[i] - 10.0 * scratch[i][...] - e3[i]).astype(BF16) for i in sides]
    tail = [mm(e3[i].astype(BF16), inner[i]) for i in sides]
    a, b = 1.25**2, 1.25**6
    rest = [
        -(a + b) * scratch[i][...] + (5.0 * b) * e2[i] - (10.0 * b) * e3[i] - b * tail[i]
        for i in sides
    ]
    return [one.astype(BF16) for one in rest], [lax.rsqrt(jnp.sqrt(norm)) for norm in norms]


def step_kernel(
    due_hbm, grad_hbm, weight_hbm, sl_hbm, sr_hbm, rl_hbm, rr_hbm,
    nl_hbm, nr_hbm, update_ref, new_ref,
    due_ref, grad_ref, weight_ref, sl, sr, left, right, cond_ref, sems,
):
    copy = pltpu.make_async_copy
    get_grad = copy(grad_hbm, grad_ref, sems.at[0])
    get_sl = copy(sl_hbm, sl, sems.at[1])
    get_sr = copy(sr_hbm, sr, sems.at[2])
    get_weight = copy(weight_hbm, weight_ref, sems.at[3])
    get_rl = copy(rl_hbm, left, sems.at[4])
    get_rr = copy(rr_hbm, right, sems.at[5])
    put_sl = copy(sl, nl_hbm, sems.at[6])
    put_sr = copy(sr, nr_hbm, sems.at[7])
    get_due = copy(due_hbm, due_ref, sems.at[8])
    get_grad.start()
    get_due.start()
    get_sl.start()
    get_sr.start()
    get_weight.start()
    row = lax.axis_index("x") * 8 + lax.axis_index("z")
    col = lax.axis_index("y") * 2 + lax.axis_index("core")
    get_grad.wait()
    get_due.wait()
    due = due_ref[col, row % 16] == row

    @pl.when(jnp.logical_not(due))
    def _():
        get_rl.start()
        get_rr.start()

    grad = grad_ref[...]
    count = 1.0 / (BLOCK * BLOCK)
    grad_norm = jnp.sqrt(total(jnp.square(grad.astype(F32))) * count)
    scale = (1.0 - KEEP) / BLOCK
    gram = lax.dot_general(grad, grad, (((1,), (1,)), ((), ())), preferred_element_type=F32)
    get_sl.wait()
    sl[...] = KEEP * sl[...] + scale * gram
    put_sl.start()
    gram = lax.dot_general(grad, grad, (((0,), (0,)), ((), ())), preferred_element_type=F32)
    get_sr.wait()
    sr[...] = KEEP * sr[...] + scale * gram
    put_sr.start()

    @pl.when(due)
    def _():
        rest, scale = fresh_roots((sl, sr), (left, right))
        half = (1.25**2 * grad.astype(F32) + mm(rest[0], grad)) * scale[0]
        cond_ref[...] = (1.25**2 * half + mm(half.astype(BF16), rest[1])) * scale[1]

    @pl.when(jnp.logical_not(due))
    def _():
        get_rl.wait()
        get_rr.wait()
        on_diagonal = unit(BLOCK)
        used = left[...]
        diag = jnp.sum(jnp.where(on_diagonal, used, 0.0), axis=1, keepdims=True)
        half = diag * grad.astype(F32) + mm(jnp.where(on_diagonal, 0.0, used).astype(BF16), grad)
        used = right[...]
        diag = jnp.sum(jnp.where(on_diagonal, used, 0.0), axis=0, keepdims=True)
        off = jnp.where(on_diagonal, 0.0, used).astype(BF16)
        cond_ref[...] = half * diag + mm(half.astype(BF16), off)

    cond = cond_ref[...]
    graft = grad_norm / jnp.sqrt(total(cond * cond) * count + FLOOR)
    update = (cond * graft).astype(BF16)
    update_ref[...] = update
    get_weight.wait()
    new_ref[...] = (weight_ref[...].astype(F32) - STEP * update.astype(F32)).astype(BF16)
    put_sl.wait()
    put_sr.wait()


def block_step(*operands):
    wide = jax.ShapeDtypeStruct((BLOCK, BLOCK), F32)
    low = jax.ShapeDtypeStruct((BLOCK, BLOCK), BF16)
    return pl.pallas_call(
        step_kernel,
        out_shape=(wide, wide, pltpu.VMEM((BLOCK, BLOCK), BF16), pltpu.VMEM((BLOCK, BLOCK), BF16)),
        in_specs=[HBM] * 7,
        out_specs=(HBM, HBM, VMEM, VMEM),
        scratch_shapes=[pltpu.SMEM((8, 16), jnp.int32)]
        + [pltpu.VMEM((BLOCK, BLOCK), BF16) for _ in range(2)]
        + [pltpu.VMEM((BLOCK, BLOCK), F32) for _ in range(5)]
        + [pltpu.SemaphoreType.DMA((9,))],
        compiler_params=pltpu.CompilerParams(vmem_limit_bytes=24 * 1024 * 1024),
        cost_estimate=pl.CostEstimate(
            flops=2 * 30 * BLOCK**3, bytes_accessed=9 * 1024 * 1024, transcendentals=0
        ),
        name="block_step",
    )(*[hbm(one) for one in operands])


def split_kernel(hidden, *outs):
    place = lax.axis_index("z") % 4
    for shift in range(4):
        start = pl.multiple_of(((place + shift) % 4) * BLOCK, BLOCK)
        outs[shift][...] = hidden[:, pl.ds(start, BLOCK)]


def split_hidden(hidden):
    part = pltpu.VMEM((ROWS, BLOCK), BF16)
    return pl.pallas_call(
        split_kernel,
        out_shape=(part,) * 4,
        in_specs=[VMEM],
        out_specs=(VMEM,) * 4,
        compiler_params=pltpu.CompilerParams(vmem_limit_bytes=4 * 1024 * 1024),
        cost_estimate=pl.CostEstimate(flops=0, bytes_accessed=1024 * 1024, transcendentals=0),
        name="split_hidden",
    )(hidden)


def multiply(acc, blocks, placed):
    y = lax.axis_index("y")
    for j in range(1, 4):
        acc += mm(blocks[j - 1][...], placed[(y + j) % 4])
    return acc


def near_kernel(*refs):
    near, far, weights = refs[0:4], refs[4], refs[5:10]
    near_sum, far_sum, placed, sems = refs[10:14]
    x, y = lax.axis_index("x"), lax.axis_index("y")
    opposite = placed.at[(x + 2) % 4]
    homes = [
        placed.at[x],
        placed.at[(x + 1) % 4],
        opposite.at[pl.ds(0, HALF)],
        opposite.at[pl.ds(HALF, HALF)],
        placed.at[(x + 3) % 4],
    ]
    copies = [pltpu.make_async_copy(weights[i], homes[i], sems.at[i]) for i in range(5)]
    for one in copies:
        one.start()
    for one in copies:
        one.wait()
    near_sum[...] = multiply(mm(near[0][...], placed[y]), near[1:], placed)
    far_sum[...] = mm(far[...], placed[y])


def project_near(near, far, weights):
    wide = pltpu.VMEM((BLOCK, BLOCK), F32)
    return pl.pallas_call(
        near_kernel,
        out_shape=(wide, wide, pltpu.VMEM((4, BLOCK, BLOCK), BF16)),
        in_specs=[VMEM] * 10,
        out_specs=(VMEM,) * 3,
        scratch_shapes=[pltpu.SemaphoreType.DMA((5,))],
        compiler_params=pltpu.CompilerParams(vmem_limit_bytes=16 * 1024 * 1024),
        cost_estimate=pl.CostEstimate(
            flops=2 * 512 * 2048 * BLOCK, bytes_accessed=7 * 1024 * 1024, transcendentals=0
        ),
        name="project_near",
    )(*[vmem(one) for one in (*near, far, *weights)])


def far_kernel(*refs):
    far, near_sum, far_part, placed, outs = refs[0:3], refs[3], refs[4], refs[5], refs[6:14]
    z, core = lax.axis_index("z"), lax.axis_index("core")
    far_sum = multiply(far_part[...], far, placed)
    for s in range(8):
        piece = -s % 4
        rows = slice(piece * ROWS, (piece + 1) * ROWS)
        is_near = ((z + s) % 8) // 4 == core
        outs[s][...] = jnp.where(is_near, near_sum[rows], far_sum[rows]).astype(outs[s].dtype)


def project_far(far, near_sum, far_part, placed):
    part = pltpu.VMEM((ROWS, BLOCK), BF16)
    return pl.pallas_call(
        far_kernel,
        out_shape=(pltpu.VMEM((ROWS, BLOCK), F32),) + (part,) * 7,
        in_specs=[VMEM] * 6,
        out_specs=(VMEM,) * 8,
        compiler_params=pltpu.CompilerParams(vmem_limit_bytes=16 * 1024 * 1024),
        cost_estimate=pl.CostEstimate(
            flops=2 * 512 * 2048 * BLOCK, bytes_accessed=7 * 1024 * 1024, transcendentals=0
        ),
        name="project_far",
    )(*[vmem(one) for one in (*far, near_sum, far_part, placed)])


def ring(size, shift):
    return [((i + shift) % size, i) for i in range(size)]


def add(first, second):
    return (first.astype(F32) + second.astype(F32)).astype(BF16)


def body(hidden, weight, gradient, stats_left, stats_right, root_left, root_right, due_rows):
    pieces = split_hidden(hidden)
    tokens = []
    for shift in range(4):
        perm = []
        for z in range(8):
            for core in range(2):
                perm.append((z * 2 + core, (core * 4 + (z % 4 + shift) % 4) * 2 + z // 4))
        tokens.append(lax.ppermute(pieces[shift], ("z", "core"), perm))
    new_left, new_right, update, new_weight = block_step(
        due_rows.T, gradient, weight, stats_left, stats_right, root_left, root_right
    )
    *tokens, _ = lax.optimization_barrier((*tokens, new_weight))
    own = jnp.concatenate(tokens, axis=0)
    near = [own] + [lax.ppermute(own, "y", ring(4, j)) for j in (1, 2, 3)]
    one, three = (lax.ppermute(new_weight, "x", ring(4, i)) for i in (1, 3))
    top = lax.ppermute(one[:HALF], "x", ring(4, 1))
    bottom = lax.ppermute(three[HALF:], "x", ring(4, 3))
    near[1], top, bottom = lax.optimization_barrier((near[1], top, bottom))
    weights = [new_weight, one, top, bottom, three]
    far = [lax.ppermute(piece, "core", ring(2, 1)) for piece in near]
    parts = project_far(far[1:], *project_near(near, far[0], weights))
    up, down = parts[3], parts[5]
    for near_up, near_down in ((parts[2], parts[6]), (parts[1], parts[7])):
        up = add(near_up, lax.ppermute(up, "z", ring(8, 7)))
        down = add(near_down, lax.ppermute(down, "z", ring(8, 1)))
    up, down = lax.ppermute(up, "z", ring(8, 7)), lax.ppermute(down, "z", ring(8, 1))
    far_sum = lax.ppermute(parts[4], "z", ring(8, 4))
    projected = parts[0] + up.astype(F32) + down.astype(F32) + far_sum.astype(F32)
    return (new_left, new_right, update, projected.astype(BF16))


def solution(mesh):
    grid = Mesh(mesh.devices.reshape(4, 8, 4, 2), ("x", "z", "y", "core"))
    spec = P(("x", "z"), ("y", "core"))
    return jax.shard_map(
        body,
        mesh=grid,
        in_specs=(spec,) * 7 + (P(),),
        out_specs=(spec,) * 4,
        check_vma=False,
    )
```

```python
import jax
import jax.numpy as jnp
from jax import lax
from jax.experimental import pallas as pl
from jax.experimental.pallas import tpu as pltpu
from jax.sharding import Mesh, PartitionSpec as P

BLOCK = 512
HALF = 256
ROWS = 128
RIDGE = 0.001
KEEP = 0.75
STEP = 0.003
FLOOR = 1e-06
F32 = jnp.float32
BF16 = jnp.bfloat16
HBM = pl.BlockSpec(memory_space=pltpu.HBM)
VMEM = pl.BlockSpec(memory_space=pltpu.VMEM)


def vmem(one):
    return pltpu.with_memory_space_constraint(one, pltpu.VMEM)


def hbm(one):
    return pltpu.with_memory_space_constraint(one, pltpu.HBM)


def mm(first, second):
    return jnp.dot(first, second, preferred_element_type=F32)


def total(values):
    return jnp.sum(jnp.sum(values, axis=0, keepdims=True), axis=1, keepdims=True)


def unit(size):
    rows = lax.broadcasted_iota(jnp.int32, (size, size), 0)
    cols = lax.broadcasted_iota(jnp.int32, (size, size), 1)
    return rows == cols


def tiles():
    return [(slice(i, i + ROWS), slice(i, i + ROWS)) for i in range(0, BLOCK, ROWS)]


def fresh_roots(statistics, scratch):
    diagonal = unit(ROWS)
    sides = range(len(statistics))
    norms = []
    for statistic in statistics:
        values = statistic[...]
        trace = sum(total(jnp.where(diagonal, statistic[tile], 0.0)) for tile in tiles())
        squares = total(values * values)
        norms.append(jnp.sqrt(squares + 2.0 * RIDGE * trace + BLOCK * RIDGE * RIDGE))
    for i in sides:
        shrink = 0.2 / norms[i]
        scratch[i][...] = statistics[i][...] * shrink
        for tile in tiles():
            scratch[i][tile] += jnp.where(diagonal, RIDGE * shrink, 0.0)
    low = [scratch[i][...].astype(BF16) for i in sides]
    e2 = [mm(low[i], low[i]) for i in sides]
    e3 = [mm(e2[i].astype(BF16), low[i]) for i in sides]
    inner = [(5.0 * e2[i] - 10.0 * scratch[i][...] - e3[i]).astype(BF16) for i in sides]
    tail = [mm(e3[i].astype(BF16), inner[i]) for i in sides]
    a, b = 1.25**2, 1.25**6
    rest = [
        -(a + b) * scratch[i][...] + (5.0 * b) * e2[i] - (10.0 * b) * e3[i] - b * tail[i]
        for i in sides
    ]
    return [one.astype(BF16) for one in rest], [lax.rsqrt(jnp.sqrt(norm)) for norm in norms]


def step_kernel(
    due_hbm, grad_hbm, weight_hbm, sl_hbm, sr_hbm, rl_hbm, rr_hbm,
    nl_hbm, nr_hbm, update_ref, new_ref,
    due_ref, grad_ref, weight_ref, sl, sr, left, right, cond_ref, sems,
):
    copy = pltpu.make_async_copy
    get_grad = copy(grad_hbm, grad_ref, sems.at[0])
    get_sl = copy(sl_hbm, sl, sems.at[1])
    get_sr = copy(sr_hbm, sr, sems.at[2])
    get_weight = copy(weight_hbm, weight_ref, sems.at[3])
    get_rl = copy(rl_hbm, left, sems.at[4])
    get_rr = copy(rr_hbm, right, sems.at[5])
    put_sl = copy(sl, nl_hbm, sems.at[6])
    put_sr = copy(sr, nr_hbm, sems.at[7])
    get_due = copy(due_hbm, due_ref, sems.at[8])
    get_grad.start()
    get_due.start()
    get_sl.start()
    get_sr.start()
    get_weight.start()
    row = lax.axis_index("x") * 8 + lax.axis_index("z")
    col = lax.axis_index("y") * 2 + lax.axis_index("core")
    get_grad.wait()
    get_due.wait()
    due = due_ref[col, row % 16] == row

    @pl.when(jnp.logical_not(due))
    def _():
        get_rl.start()
        get_rr.start()

    grad = grad_ref[...]
    count = 1.0 / (BLOCK * BLOCK)
    grad_norm = jnp.sqrt(total(jnp.square(grad.astype(F32))) * count)
    scale = (1.0 - KEEP) / BLOCK
    gram = lax.dot_general(grad, grad, (((1,), (1,)), ((), ())), preferred_element_type=F32)
    get_sl.wait()
    sl[...] = KEEP * sl[...] + scale * gram
    put_sl.start()
    gram = lax.dot_general(grad, grad, (((0,), (0,)), ((), ())), preferred_element_type=F32)
    get_sr.wait()
    sr[...] = KEEP * sr[...] + scale * gram
    put_sr.start()

    @pl.when(due)
    def _():
        rest, scale = fresh_roots((sl, sr), (left, right))
        half = (1.25**2 * grad.astype(F32) + mm(rest[0], grad)) * scale[0]
        cond_ref[...] = (1.25**2 * half + mm(half.astype(BF16), rest[1])) * scale[1]

    @pl.when(jnp.logical_not(due))
    def _():
        get_rl.wait()
        get_rr.wait()
        on_diagonal = unit(BLOCK)
        used = left[...]
        diag = jnp.sum(jnp.where(on_diagonal, used, 0.0), axis=1, keepdims=True)
        half = diag * grad.astype(F32) + mm(jnp.where(on_diagonal, 0.0, used).astype(BF16), grad)
        used = right[...]
        diag = jnp.sum(jnp.where(on_diagonal, used, 0.0), axis=0, keepdims=True)
        off = jnp.where(on_diagonal, 0.0, used).astype(BF16)
        cond_ref[...] = half * diag + mm(half.astype(BF16), off)

    cond = cond_ref[...]
    graft = grad_norm / jnp.sqrt(total(cond * cond) * count + FLOOR)
    update = (cond * graft).astype(BF16)
    update_ref[...] = update
    get_weight.wait()
    new_ref[...] = (weight_ref[...].astype(F32) - STEP * update.astype(F32)).astype(BF16)
    put_sl.wait()
    put_sr.wait()


def block_step(*operands):
    wide = jax.ShapeDtypeStruct((BLOCK, BLOCK), F32)
    low = jax.ShapeDtypeStruct((BLOCK, BLOCK), BF16)
    return pl.pallas_call(
        step_kernel,
        out_shape=(wide, wide, pltpu.VMEM((BLOCK, BLOCK), BF16), pltpu.VMEM((BLOCK, BLOCK), BF16)),
        in_specs=[HBM] * 7,
        out_specs=(HBM, HBM, VMEM, VMEM),
        scratch_shapes=[pltpu.SMEM((8, 16), jnp.int32)]
        + [pltpu.VMEM((BLOCK, BLOCK), BF16) for _ in range(2)]
        + [pltpu.VMEM((BLOCK, BLOCK), F32) for _ in range(5)]
        + [pltpu.SemaphoreType.DMA((9,))],
        compiler_params=pltpu.CompilerParams(vmem_limit_bytes=24 * 1024 * 1024),
        cost_estimate=pl.CostEstimate(
            flops=2 * 30 * BLOCK**3, bytes_accessed=9 * 1024 * 1024, transcendentals=0
        ),
        name="block_step",
    )(*[hbm(one) for one in operands])


def split_kernel(hidden, *outs):
    place = lax.axis_index("z") % 4
    for shift in range(4):
        start = pl.multiple_of(((place + shift) % 4) * BLOCK, BLOCK)
        outs[shift][...] = hidden[:, pl.ds(start, BLOCK)]


def split_hidden(hidden):
    part = pltpu.VMEM((ROWS, BLOCK), BF16)
    return pl.pallas_call(
        split_kernel,
        out_shape=(part,) * 4,
        in_specs=[VMEM],
        out_specs=(VMEM,) * 4,
        compiler_params=pltpu.CompilerParams(vmem_limit_bytes=4 * 1024 * 1024),
        cost_estimate=pl.CostEstimate(flops=0, bytes_accessed=1024 * 1024, transcendentals=0),
        name="split_hidden",
    )(hidden)


def multiply(acc, blocks, placed):
    y = lax.axis_index("y")
    for j in range(1, 4):
        acc += mm(blocks[j - 1][...], placed[(y + j) % 4])
    return acc


def near_kernel(*refs):
    near, far, weights = refs[0:4], refs[4], refs[5:10]
    near_sum, far_sum, placed, sems = refs[10:14]
    x, y = lax.axis_index("x"), lax.axis_index("y")
    opposite = placed.at[(x + 2) % 4]
    homes = [
        placed.at[x],
        placed.at[(x + 1) % 4],
        opposite.at[pl.ds(0, HALF)],
        opposite.at[pl.ds(HALF, HALF)],
        placed.at[(x + 3) % 4],
    ]
    copies = [pltpu.make_async_copy(weights[i], homes[i], sems.at[i]) for i in range(5)]
    for one in copies:
        one.start()
    for one in copies:
        one.wait()
    near_sum[...] = multiply(mm(near[0][...], placed[y]), near[1:], placed)
    far_sum[...] = mm(far[...], placed[y])


def project_near(near, far, weights):
    wide = pltpu.VMEM((BLOCK, BLOCK), F32)
    return pl.pallas_call(
        near_kernel,
        out_shape=(wide, wide, pltpu.VMEM((4, BLOCK, BLOCK), BF16)),
        in_specs=[VMEM] * 10,
        out_specs=(VMEM,) * 3,
        scratch_shapes=[pltpu.SemaphoreType.DMA((5,))],
        compiler_params=pltpu.CompilerParams(vmem_limit_bytes=16 * 1024 * 1024),
        cost_estimate=pl.CostEstimate(
            flops=2 * 512 * 2048 * BLOCK, bytes_accessed=7 * 1024 * 1024, transcendentals=0
        ),
        name="project_near",
    )(*[vmem(one) for one in (*near, far, *weights)])


def far_kernel(*refs):
    far, near_sum, far_part, placed, outs = refs[0:3], refs[3], refs[4], refs[5], refs[6:14]
    z, core = lax.axis_index("z"), lax.axis_index("core")
    far_sum = multiply(far_part[...], far, placed)
    for s in range(8):
        piece = -s % 4
        rows = slice(piece * ROWS, (piece + 1) * ROWS)
        is_near = ((z + s) % 8) // 4 == core
        outs[s][...] = jnp.where(is_near, near_sum[rows], far_sum[rows]).astype(outs[s].dtype)


def project_far(far, near_sum, far_part, placed):
    part = pltpu.VMEM((ROWS, BLOCK), BF16)
    return pl.pallas_call(
        far_kernel,
        out_shape=(pltpu.VMEM((ROWS, BLOCK), F32),) + (part,) * 7,
        in_specs=[VMEM] * 6,
        out_specs=(VMEM,) * 8,
        compiler_params=pltpu.CompilerParams(vmem_limit_bytes=16 * 1024 * 1024),
        cost_estimate=pl.CostEstimate(
            flops=2 * 512 * 2048 * BLOCK, bytes_accessed=7 * 1024 * 1024, transcendentals=0
        ),
        name="project_far",
    )(*[vmem(one) for one in (*far, near_sum, far_part, placed)])


def ring(size, shift):
    return [((i + shift) % size, i) for i in range(size)]


def add(first, second):
    return (first.astype(F32) + second.astype(F32)).astype(BF16)


def body(hidden, weight, gradient, stats_left, stats_right, root_left, root_right, due_rows):
    pieces = split_hidden(hidden)
    tokens = []
    for shift in range(4):
        perm = []
        for z in range(8):
            for core in range(2):
                perm.append((z * 2 + core, (core * 4 + (z % 4 + shift) % 4) * 2 + z // 4))
        tokens.append(lax.ppermute(pieces[shift], ("z", "core"), perm))
    new_left, new_right, update, new_weight = block_step(
        due_rows.T, gradient, weight, stats_left, stats_right, root_left, root_right
    )
    *tokens, _ = lax.optimization_barrier((*tokens, new_weight))
    own = jnp.concatenate(tokens, axis=0)
    near = [own] + [lax.ppermute(own, "y", ring(4, j)) for j in (1, 2, 3)]
    one, three = (lax.ppermute(new_weight, "x", ring(4, i)) for i in (1, 3))
    top = lax.ppermute(one[:HALF], "x", ring(4, 1))
    bottom = lax.ppermute(three[HALF:], "x", ring(4, 3))
    near[2], top, bottom = lax.optimization_barrier((near[2], top, bottom))
    weights = [new_weight, one, top, bottom, three]
    far = [lax.ppermute(piece, "core", ring(2, 1)) for piece in near]
    parts = project_far(far[1:], *project_near(near, far[0], weights))
    up, down = parts[3], parts[5]
    for near_up, near_down in ((parts[2], parts[6]), (parts[1], parts[7])):
        up = add(near_up, lax.ppermute(up, "z", ring(8, 7)))
        down = add(near_down, lax.ppermute(down, "z", ring(8, 1)))
    up, down = lax.ppermute(up, "z", ring(8, 7)), lax.ppermute(down, "z", ring(8, 1))
    far_sum = lax.ppermute(parts[4], "z", ring(8, 4))
    projected = parts[0] + up.astype(F32) + down.astype(F32) + far_sum.astype(F32)
    return (new_left, new_right, update, projected.astype(BF16))


def solution(mesh):
    grid = Mesh(mesh.devices.reshape(4, 8, 4, 2), ("x", "z", "y", "core"))
    spec = P(("x", "z"), ("y", "core"))
    return jax.shard_map(
        body,
        mesh=grid,
        in_specs=(spec,) * 7 + (P(),),
        out_specs=(spec,) * 4,
        check_vma=False,
    )
```

```python
import functools

import jax
import jax.numpy as jnp
from jax import lax
from jax.experimental import pallas as pl
from jax.experimental.pallas import tpu as pltpu
from jax.sharding import Mesh, PartitionSpec as P

BLOCK = 512
HALF = 256
ROWS = 128
RIDGE = 0.001
KEEP = 0.75
STEP = 0.003
FLOOR = 1e-06
SENDS = {(1, 3): (3, 7, 1, 5), (0, 2): (0, 4, 2, 6)}
F32 = jnp.float32
BF16 = jnp.bfloat16
HBM = pl.BlockSpec(memory_space=pltpu.HBM)
VMEM = pl.BlockSpec(memory_space=pltpu.VMEM)


def vmem(one):
    return pltpu.with_memory_space_constraint(one, pltpu.VMEM)


def hbm(one):
    return pltpu.with_memory_space_constraint(one, pltpu.HBM)


def mm(first, second):
    return jnp.dot(first, second, preferred_element_type=F32)


def total(values):
    return jnp.sum(jnp.sum(values, axis=0, keepdims=True), axis=1, keepdims=True)


def unit(size):
    rows = lax.broadcasted_iota(jnp.int32, (size, size), 0)
    cols = lax.broadcasted_iota(jnp.int32, (size, size), 1)
    return rows == cols


def tiles():
    return [(slice(i, i + ROWS), slice(i, i + ROWS)) for i in range(0, BLOCK, ROWS)]


def fresh_roots(statistics, scratch):
    diagonal = unit(ROWS)
    sides = range(len(statistics))
    norms = []
    for statistic in statistics:
        values = statistic[...]
        trace = sum(total(jnp.where(diagonal, statistic[tile], 0.0)) for tile in tiles())
        squares = total(values * values)
        norms.append(jnp.sqrt(squares + 2.0 * RIDGE * trace + BLOCK * RIDGE * RIDGE))
    for i in sides:
        shrink = 0.2 / norms[i]
        scratch[i][...] = statistics[i][...] * shrink
        for tile in tiles():
            scratch[i][tile] += jnp.where(diagonal, RIDGE * shrink, 0.0)
    low = [scratch[i][...].astype(BF16) for i in sides]
    e2 = [mm(low[i], low[i]) for i in sides]
    e3 = [mm(e2[i].astype(BF16), low[i]) for i in sides]
    inner = [(5.0 * e2[i] - 10.0 * scratch[i][...] - e3[i]).astype(BF16) for i in sides]
    tail = [mm(e3[i].astype(BF16), inner[i]) for i in sides]
    a, b = 1.25**2, 1.25**6
    rest = [
        -(a + b) * scratch[i][...] + (5.0 * b) * e2[i] - (10.0 * b) * e3[i] - b * tail[i]
        for i in sides
    ]
    return [one.astype(BF16) for one in rest], [lax.rsqrt(jnp.sqrt(norm)) for norm in norms]


def step_kernel(
    due_hbm, grad_hbm, weight_hbm, sl_hbm, sr_hbm, rl_hbm, rr_hbm,
    nl_hbm, nr_hbm, update_ref, new_ref,
    due_ref, grad_ref, weight_ref, sl, sr, left, right, cond_ref, sems,
):
    copy = pltpu.make_async_copy
    get_grad = copy(grad_hbm, grad_ref, sems.at[0])
    get_sl = copy(sl_hbm, sl, sems.at[1])
    get_sr = copy(sr_hbm, sr, sems.at[2])
    get_weight = copy(weight_hbm, weight_ref, sems.at[3])
    get_rl = copy(rl_hbm, left, sems.at[4])
    get_rr = copy(rr_hbm, right, sems.at[5])
    put_sl = copy(sl, nl_hbm, sems.at[6])
    put_sr = copy(sr, nr_hbm, sems.at[7])
    get_due = copy(due_hbm, due_ref, sems.at[8])
    get_grad.start()
    get_due.start()
    get_sl.start()
    get_sr.start()
    get_weight.start()
    row = lax.axis_index("x") * 8 + lax.axis_index("z")
    col = lax.axis_index("y") * 2 + lax.axis_index("core")
    get_grad.wait()
    get_due.wait()
    due = due_ref[col, row % 16] == row

    @pl.when(jnp.logical_not(due))
    def _():
        get_rl.start()
        get_rr.start()

    grad = grad_ref[...]
    count = 1.0 / (BLOCK * BLOCK)
    grad_norm = jnp.sqrt(total(jnp.square(grad.astype(F32))) * count)
    scale = (1.0 - KEEP) / BLOCK
    gram = lax.dot_general(grad, grad, (((1,), (1,)), ((), ())), preferred_element_type=F32)
    get_sl.wait()
    sl[...] = KEEP * sl[...] + scale * gram
    put_sl.start()
    gram = lax.dot_general(grad, grad, (((0,), (0,)), ((), ())), preferred_element_type=F32)
    get_sr.wait()
    sr[...] = KEEP * sr[...] + scale * gram
    put_sr.start()

    @pl.when(due)
    def _():
        rest, scale = fresh_roots((sl, sr), (left, right))
        half = (1.25**2 * grad.astype(F32) + mm(rest[0], grad)) * scale[0]
        cond_ref[...] = (1.25**2 * half + mm(half.astype(BF16), rest[1])) * scale[1]

    @pl.when(jnp.logical_not(due))
    def _():
        get_rl.wait()
        get_rr.wait()
        on_diagonal = unit(BLOCK)
        used = left[...]
        diag = jnp.sum(jnp.where(on_diagonal, used, 0.0), axis=1, keepdims=True)
        half = diag * grad.astype(F32) + mm(jnp.where(on_diagonal, 0.0, used).astype(BF16), grad)
        used = right[...]
        diag = jnp.sum(jnp.where(on_diagonal, used, 0.0), axis=0, keepdims=True)
        off = jnp.where(on_diagonal, 0.0, used).astype(BF16)
        cond_ref[...] = half * diag + mm(half.astype(BF16), off)

    cond = cond_ref[...]
    graft = grad_norm / jnp.sqrt(total(cond * cond) * count + FLOOR)
    update = (cond * graft).astype(BF16)
    update_ref[...] = update
    get_weight.wait()
    new_ref[...] = (weight_ref[...].astype(F32) - STEP * update.astype(F32)).astype(BF16)
    put_sl.wait()
    put_sr.wait()


def block_step(*operands):
    wide = jax.ShapeDtypeStruct((BLOCK, BLOCK), F32)
    low = jax.ShapeDtypeStruct((BLOCK, BLOCK), BF16)
    return pl.pallas_call(
        step_kernel,
        out_shape=(wide, wide, pltpu.VMEM((BLOCK, BLOCK), BF16), pltpu.VMEM((BLOCK, BLOCK), BF16)),
        in_specs=[HBM] * 7,
        out_specs=(HBM, HBM, VMEM, VMEM),
        scratch_shapes=[pltpu.SMEM((8, 16), jnp.int32)]
        + [pltpu.VMEM((BLOCK, BLOCK), BF16) for _ in range(2)]
        + [pltpu.VMEM((BLOCK, BLOCK), F32) for _ in range(5)]
        + [pltpu.SemaphoreType.DMA((9,))],
        compiler_params=pltpu.CompilerParams(vmem_limit_bytes=24 * 1024 * 1024),
        cost_estimate=pl.CostEstimate(
            flops=2 * 30 * BLOCK**3, bytes_accessed=9 * 1024 * 1024, transcendentals=0
        ),
        name="block_step",
    )(*[hbm(one) for one in operands])


def split_kernel(hidden, *outs):
    place = lax.axis_index("z") % 4
    for shift in range(4):
        start = pl.multiple_of(((place + shift) % 4) * BLOCK, BLOCK)
        outs[shift][...] = hidden[:, pl.ds(start, BLOCK)]


def split_hidden(hidden):
    part = pltpu.VMEM((ROWS, BLOCK), BF16)
    return pl.pallas_call(
        split_kernel,
        out_shape=(part,) * 4,
        in_specs=[VMEM],
        out_specs=(VMEM,) * 4,
        compiler_params=pltpu.CompilerParams(vmem_limit_bytes=4 * 1024 * 1024),
        cost_estimate=pl.CostEstimate(flops=0, bytes_accessed=1024 * 1024, transcendentals=0),
        name="split_hidden",
    )(hidden)


def multiply(acc, blocks, placed):
    y = lax.axis_index("y")
    for j in range(1, 4):
        acc += mm(blocks[j - 1][...], placed[(y + j) % 4])
    return acc


def near_kernel(*refs):
    near, far, weights = refs[0:4], refs[4], refs[5:10]
    near_sum, far_sum, placed, sems = refs[10:14]
    x, y = lax.axis_index("x"), lax.axis_index("y")
    opposite = placed.at[(x + 2) % 4]
    homes = [
        placed.at[x],
        placed.at[(x + 1) % 4],
        opposite.at[pl.ds(0, HALF)],
        opposite.at[pl.ds(HALF, HALF)],
        placed.at[(x + 3) % 4],
    ]
    copies = [pltpu.make_async_copy(weights[i], homes[i], sems.at[i]) for i in range(5)]
    for one in copies:
        one.start()
    for one in copies:
        one.wait()
    near_sum[...] = multiply(mm(near[0][...], placed[y]), near[1:], placed)
    far_sum[...] = mm(far[...], placed[y])


def project_near(near, far, weights):
    wide = pltpu.VMEM((BLOCK, BLOCK), F32)
    return pl.pallas_call(
        near_kernel,
        out_shape=(wide, wide, pltpu.VMEM((4, BLOCK, BLOCK), BF16)),
        in_specs=[VMEM] * 10,
        out_specs=(VMEM,) * 3,
        scratch_shapes=[pltpu.SemaphoreType.DMA((5,))],
        compiler_params=pltpu.CompilerParams(vmem_limit_bytes=16 * 1024 * 1024),
        cost_estimate=pl.CostEstimate(
            flops=2 * 512 * 2048 * BLOCK, bytes_accessed=7 * 1024 * 1024, transcendentals=0
        ),
        name="project_near",
    )(*[vmem(one) for one in (*near, far, *weights)])


def far_kernel(pieces, *refs):
    far, near_sum, far_part, placed, outs = refs[0:3], refs[3], refs[4], refs[5], refs[6:10]
    z, y, core = lax.axis_index("z"), lax.axis_index("y"), lax.axis_index("core")
    rows = [slice(piece * ROWS, (piece + 1) * ROWS) for piece in pieces]
    acc = jnp.concatenate([far_part[one] for one in rows], axis=0)
    for j in range(1, 4):
        acc += mm(jnp.concatenate([far[j - 1][one] for one in rows], axis=0), placed[(y + j) % 4])
    for k, s in enumerate(SENDS[pieces]):
        i = pieces.index(-s % 4)
        is_near = ((z + s) % 8) // 4 == core
        part = jnp.where(is_near, near_sum[rows[i]], acc[i * ROWS : (i + 1) * ROWS])
        outs[k][...] = part.astype(outs[k].dtype)


def project_far(pieces, far, near_sum, far_part, placed):
    kinds = [F32 if s == 0 else BF16 for s in SENDS[pieces]]
    parts = pl.pallas_call(
        functools.partial(far_kernel, pieces),
        out_shape=tuple(pltpu.VMEM((ROWS, BLOCK), kind) for kind in kinds),
        in_specs=[VMEM] * 6,
        out_specs=(VMEM,) * 4,
        compiler_params=pltpu.CompilerParams(vmem_limit_bytes=16 * 1024 * 1024),
        cost_estimate=pl.CostEstimate(
            flops=2 * 256 * 1536 * BLOCK, bytes_accessed=4 * 1024 * 1024, transcendentals=0
        ),
        name="project_far",
    )(*[vmem(one) for one in (*far, near_sum, far_part, placed)])
    return dict(zip(SENDS[pieces], parts))


def ring(size, shift):
    return [((i + shift) % size, i) for i in range(size)]


def add(first, second):
    return (first.astype(F32) + second.astype(F32)).astype(BF16)


def body(hidden, weight, gradient, stats_left, stats_right, root_left, root_right, due_rows):
    pieces = split_hidden(hidden)
    tokens = []
    for shift in range(4):
        perm = []
        for z in range(8):
            for core in range(2):
                perm.append((z * 2 + core, (core * 4 + (z % 4 + shift) % 4) * 2 + z // 4))
        tokens.append(lax.ppermute(pieces[shift], ("z", "core"), perm))
    new_left, new_right, update, new_weight = block_step(
        due_rows.T, gradient, weight, stats_left, stats_right, root_left, root_right
    )
    *tokens, _ = lax.optimization_barrier((*tokens, new_weight))
    own = jnp.concatenate(tokens, axis=0)
    near = [own] + [lax.ppermute(own, "y", ring(4, j)) for j in (1, 2, 3)]
    one, three = (lax.ppermute(new_weight, "x", ring(4, i)) for i in (1, 3))
    top = lax.ppermute(one[:HALF], "x", ring(4, 1))
    bottom = lax.ppermute(three[HALF:], "x", ring(4, 3))
    near[2], top, bottom = lax.optimization_barrier((near[2], top, bottom))
    weights = [new_weight, one, top, bottom, three]
    far = [lax.ppermute(piece, "core", ring(2, 1)) for piece in near]
    sums = project_near(near, far[0], weights)
    parts = project_far((1, 3), far[1:], *sums) | project_far((0, 2), far[1:], *sums)
    up, down = parts[3], parts[5]
    for near_up, near_down in ((parts[2], parts[6]), (parts[1], parts[7])):
        up = add(near_up, lax.ppermute(up, "z", ring(8, 7)))
        down = add(near_down, lax.ppermute(down, "z", ring(8, 1)))
    up, down = lax.ppermute(up, "z", ring(8, 7)), lax.ppermute(down, "z", ring(8, 1))
    far_sum = lax.ppermute(parts[4], "z", ring(8, 4))
    projected = parts[0] + up.astype(F32) + down.astype(F32) + far_sum.astype(F32)
    return (new_left, new_right, update, projected.astype(BF16))


def solution(mesh):
    grid = Mesh(mesh.devices.reshape(4, 8, 4, 2), ("x", "z", "y", "core"))
    spec = P(("x", "z"), ("y", "core"))
    return jax.shard_map(
        body,
        mesh=grid,
        in_specs=(spec,) * 7 + (P(),),
        out_specs=(spec,) * 4,
        check_vma=False,
    )
```
